32 devices in a mesh: parts: 2 (over x), dp: 2 (over core), tensor: 8 (over z, y).
Axes of the slice: x: 2, y: 2, z: 4, core: 2. Of those that a mesh axis runs over, the one named last changes fastest.
Arguments:
- query: bfloat16 [512, 8192], P(('parts', 'dp'), 'tensor'), parts along dimension 0, may hold values from -80 to 80
- step_key_value: bfloat16 [512, 8, 256], P(('parts', 'dp'), 'tensor'), parts along dimension 0, may hold values from -4 to 4, as said below
- cache: bfloat16 [512, 128, 8, 256], P(('parts', 'dp'), None, 'tensor'), parts along dimension 0, may hold values from -4 to 4, as said below
- output_projection_weight: bfloat16 [8192, 8192], P('tensor'), may hold values from -0.0625 to 0.0625
- adapter_down_weight: bfloat16 [8192, 128, 64], P('tensor', 'dp'), may hold values from -0.0625 to 0.0625
- adapter_up_weight: bfloat16 [128, 64, 8192], P('dp', None, 'tensor'), may hold values from -0.75 to 0.75
- row_adapter_index: int32 [512], P('parts'), parts along dimension 0, may hold values from 0 to 127
- adapter_storage_slot: int32 [128], replicated, may hold values from 0 to 127, each once
Outputs:
- mixed: bfloat16 [512, 8192], P(('parts', 'dp'), 'tensor'), parts along dimension 0
The draws below stay inside these ranges and needn't reach their ends.
There are 2 independent parts, one for each index of `parts`. The reference program is written for one: setup_inputs(seed, part) draws one part's arguments, and reference() takes and returns one part's arrays. A program takes and returns all parts, laid end to end along the dimension named above; an argument that names none is the same for every part. Nothing has to cross between parts.
Inputs may be any that keep to these rules, and one draw needn't show every extreme that they name: `cache`: copies c and c' are equal where c * 1 = c' * 8 // 8. `step_key_value`: copies c and c' are equal where c * 1 = c' * 8 // 8. `adapter_storage_slot`: each slot holds exactly one adapter.
All inputs are finite; a program needn't handle non-finite values.
Results may differ from the reference program's by a relative error of at most 0.0061.
Values may be sent and summed in bfloat16 or wider, within the bound.
A program may use at most 128 MiB of HBM per device.

```python
import math
import jax
import jax.numpy as jnp
import numpy as np
from jax import lax

MODEL_WIDTH = 8192
QUERY_HEADS = 64
KV_HEADS = 8
HEAD_SIZE = 128
ADAPTER_RANK = 64
ADAPTER_GROUP = 128
CTX = 128
ROWS = 256
KV_COPIES = 8


def shared_keys(key):
    distinct = jnp.clip(jax.random.normal(jax.random.fold_in(key, 101), (ROWS, CTX, KV_HEADS, 2 * HEAD_SIZE), jnp.float32), -4.0, 4.0)
    cached = jnp.repeat(distinct, KV_COPIES // KV_HEADS, axis=2)
    return cached


def draw_cache(key, part):
    cached = shared_keys(key)
    return cached.astype(jnp.bfloat16)


def draw_query(key, part):
    key = jax.random.fold_in(key, 2)
    values = jnp.clip(jax.random.normal(key, (ROWS, QUERY_HEADS * HEAD_SIZE), jnp.float32), -4.0, 4.0)
    return values.astype(jnp.bfloat16)


def draw_step_key_value(key, part):
    key = jax.random.fold_in(key, 3)
    distinct = jnp.clip(jax.random.normal(key, (ROWS, KV_HEADS, 2 * HEAD_SIZE), jnp.float32), -4.0, 4.0)
    return jnp.repeat(distinct, KV_COPIES // KV_HEADS, axis=1).astype(jnp.bfloat16)


def touch_ends(drawn, key, low, largest):
    spot = [jax.random.randint(jax.random.fold_in(key, axis), (), 0, length) for axis, length in enumerate(drawn.shape)]
    main_axis = drawn.shape.index(max(drawn.shape))
    neighbour = spot[:main_axis] + [(spot[main_axis] + 1) % drawn.shape[main_axis]] + spot[main_axis + 1:]
    return drawn.at[tuple(spot)].set(low).at[tuple(neighbour)].set(largest)


def shard_levels(rng, extent, cuts, smallest, top_value):
    gain = 1.0
    for position, shards_of in cuts:
        heights = jax.random.uniform(jax.random.fold_in(jax.random.fold_in(rng, 6), position), (shards_of,), jnp.float32, smallest / len(cuts), top_value / len(cuts))
        gain = gain * jnp.repeat(jnp.exp(heights), extent[position] // shards_of).reshape((-1,) + (1,) * (len(extent) - 1 - position))
    return gain


def rank_table(count, skew):
    portions = [(1 << 20) // math.isqrt(grade ** skew) + 1 for grade in range(1, count + 1)]
    deviation = 1 + sum(portions) // (1 << 30)
    return np.cumsum(np.array([max(1, weight // deviation) for weight in portions]))


def ranked_ids(stream_key, dims, number_of, lean):
    grid = rank_table(number_of, lean)
    lot = jax.random.randint(jax.random.fold_in(stream_key, 1), dims, 0, int(grid[number_of - 1]))
    grade = jnp.searchsorted(jnp.asarray(grid, jnp.int32), lot, side="right")
    return jax.random.permutation(jax.random.fold_in(stream_key, 2), number_of)[grade].astype(jnp.int32)


def normal_values(own_key, dims, width, reach, cuts=(), kind=jnp.bfloat16):
    array = jax.random.normal(own_key, dims, jnp.float32) * width
    if len(cuts) > 0:
        array = shard_levels(own_key, dims, cuts, -0.22, 0.18) * array
    return jnp.clip(array, min=-reach, max=reach).astype(kind)


def setup_inputs(seed: int = 0, part: int = 0) -> dict:
    seeds = jax.random.split(jax.random.key(seed), 9)
    part_keys = jax.random.split(jax.random.fold_in(seeds[8], part), 9)
    return {
        "query": draw_query(jax.random.fold_in(jax.random.fold_in(seeds[8], part), 71), part),
        "step_key_value": draw_step_key_value(jax.random.fold_in(jax.random.fold_in(seeds[8], part), 71), part),
        "cache": draw_cache(jax.random.fold_in(jax.random.fold_in(seeds[8], part), 71), part),
        "output_projection_weight": normal_values(seeds[3], (QUERY_HEADS * HEAD_SIZE, MODEL_WIDTH), (QUERY_HEADS * HEAD_SIZE) ** -0.5, 0.0625, ((0, 8),)),
        "adapter_down_weight": normal_values(seeds[4], (QUERY_HEADS * HEAD_SIZE, ADAPTER_GROUP, ADAPTER_RANK), (QUERY_HEADS * HEAD_SIZE) ** -0.5, 0.0625, ((0, 8), (1, 2))),
        "adapter_up_weight": normal_values(seeds[5], (ADAPTER_GROUP, ADAPTER_RANK, MODEL_WIDTH), ADAPTER_RANK ** -0.5, 0.75, ((0, 2), (2, 8))),
        "row_adapter_index": touch_ends(ranked_ids(part_keys[6], (ROWS,), ADAPTER_GROUP, 2), jax.random.fold_in(part_keys[6], 3), 0, ADAPTER_GROUP - 1).astype(jnp.int32),
        "adapter_storage_slot": jax.random.permutation(seeds[7], ADAPTER_GROUP).astype(jnp.int32),
    }


def attend_row(packed):
    query_row, new_row, cache_row = packed
    copies = cache_row.shape[1]
    head_width = cache_row.shape[2] // 2
    group = query_row.shape[0] // (copies * head_width)
    heads = query_row.reshape(copies, group, head_width).astype(jnp.float32)
    cached_keys = cache_row[:, :, :head_width].astype(jnp.float32)
    cached_values = cache_row[:, :, head_width:].astype(jnp.float32)
    score_scale = 1.0 / math.sqrt(head_width)
    scores = jnp.einsum('sgd,csd->sgc', heads, cached_keys) * score_scale
    own_score = jnp.einsum('sgd,sd->sg', heads, new_row[:, :head_width].astype(jnp.float32)) * score_scale
    peak = jnp.maximum(lax.optimization_barrier(jnp.max(scores, axis=-1)), own_score)
    expos = jnp.exp(scores - peak[..., None])
    own_expo = jnp.exp(own_score - peak)
    total = lax.optimization_barrier(jnp.sum(expos, axis=-1)) + own_expo
    weights = (expos / total[..., None]).astype(jnp.bfloat16)
    own_weight = (own_expo / total).astype(jnp.bfloat16)
    summed = jnp.einsum('sgc,csd->sgd', weights.astype(jnp.float32), cached_values)
    summed = summed + own_weight.astype(jnp.float32)[..., None] * new_row[:, None, head_width:].astype(jnp.float32)
    return summed.astype(jnp.bfloat16).reshape(-1)

def reference(query, step_key_value, cache, output_projection_weight, adapter_down_weight, adapter_up_weight, row_adapter_index, adapter_storage_slot):
    attention_result = lax.map(attend_row, (query, step_key_value, cache))
    base = jnp.dot(attention_result, output_projection_weight, preferred_element_type=jnp.float32)
    slot = adapter_storage_slot[row_adapter_index].astype(jnp.int32)
    input_feature_count = adapter_down_weight.shape[0]
    gathered_low_rank = jnp.dot(attention_result, adapter_down_weight.reshape(input_feature_count, -1), preferred_element_type=jnp.float32)
    gathered_low_rank = gathered_low_rank.reshape(attention_result.shape[0], ADAPTER_GROUP, ADAPTER_RANK)
    low = jnp.take_along_axis(gathered_low_rank, slot[:, None, None], axis=1)[:, 0, :].astype(jnp.bfloat16)
    one_hot = slot[:, None] == jnp.arange(ADAPTER_GROUP, dtype=jnp.int32)[None, :]
    widened_rows = jnp.where(one_hot[:, :, None], low[:, None, :], jnp.zeros((), jnp.bfloat16))
    widened_rows = widened_rows.reshape(attention_result.shape[0], ADAPTER_GROUP * ADAPTER_RANK)
    adapter_update = jnp.dot(widened_rows, adapter_up_weight.reshape(ADAPTER_GROUP * ADAPTER_RANK, -1), preferred_element_type=jnp.float32)
    return (base + adapter_update).astype(jnp.bfloat16)
```

```python
import functools
import math

import jax
import jax.numpy as jnp
from jax import lax
from jax.experimental import pallas as pl
from jax.experimental.pallas import tpu as pltpu
from jax.sharding import PartitionSpec as P

MESH = pl.DeviceIdType.MESH


def attend(query, step_key_value, cache):
    row_count = query.shape[0]
    copies = cache.shape[2]
    head_width = cache.shape[3] // 2
    group = query.shape[1] // (copies * head_width)
    heads = query.reshape(row_count, copies, group, head_width)
    score_scale = 1.0 / math.sqrt(head_width)
    scores = (
        jnp.einsum(
            "rsgd,rcsd->rsgc", heads, cache[..., :head_width], preferred_element_type=jnp.float32
        )
        * score_scale
    )
    own_score = (
        jnp.einsum(
            "rsgd,rsd->rsg",
            heads,
            step_key_value[..., :head_width],
            preferred_element_type=jnp.float32,
        )
        * score_scale
    )
    peak = jnp.maximum(jnp.max(scores, axis=-1), own_score)
    expos = jnp.exp(scores - peak[..., None])
    own_expo = jnp.exp(own_score - peak)
    total = jnp.sum(expos, axis=-1) + own_expo
    weights = (expos / total[..., None]).astype(jnp.bfloat16)
    own_weight = (own_expo / total).astype(jnp.bfloat16)
    summed = jnp.einsum(
        "rsgc,rcsd->rsgd", weights, cache[..., head_width:], preferred_element_type=jnp.float32
    )
    summed = summed + own_weight.astype(jnp.float32)[..., None] * step_key_value[
        :, :, None, head_width:
    ].astype(jnp.float32)
    return summed.astype(jnp.bfloat16).reshape(row_count, -1)


def flip(index, stage):
    step = 1 << stage
    bit = lax.rem(lax.div(index, step), 2)
    return index + step - 2 * step * bit


def low_stage(relative):
    return (relative & -relative).bit_length() - 1


def project(
    n, att_ref, code_ref, w_hbm, down_hbm, up_hbm, out_ref,
    w_buf, down_buf, up_buf, rows_all, send_buf, recv_buf, low_send, low_recv,
    delta, delta_send, delta_recv,
    w_sem, down_sem, up_sem, send_sem, recv_sem, low_ssem, low_rsem, pair_ssem, pair_rsem,
):
    stages = n.bit_length() - 1
    t = lax.axis_index("tensor")
    other_core = 1 - lax.axis_index("dp")
    rows, width = att_ref.shape[0], out_ref.shape[1]
    pieces, piece = down_sem.shape[0], down_buf.shape[0] // down_sem.shape[0]
    tile = min(width, 512)
    half = 64

    def load_w(x):
        block = t
        for s in range(stages):
            if (x >> s) & 1:
                block = flip(block, s)
        return pltpu.make_async_copy(
            w_hbm.at[:, pl.ds(pl.multiple_of(block * width, width), width)],
            w_buf.at[x],
            w_sem.at[x],
        )

    def load_piece(src, dst, sem, i):
        span = pl.ds(pl.multiple_of(i * piece, piece), piece)
        return pltpu.make_async_copy(src.at[span], dst.at[span], sem.at[i])

    odd = list(range(n - 1, 0, -2))
    even = list(range(n - 2, -1, -2))
    order = [odd[0]]
    for i in range(len(even) - 1):
        order += [odd[i + 1], even[i]]
    order += [0]

    load_w(order[0]).start()
    for i in range(pieces):
        load_piece(down_hbm, down_buf, down_sem, i).start()
    for x in order[1:4]:
        load_w(x).start()

    barrier = pltpu.get_barrier_semaphore()
    for s in range(stages):
        pl.semaphore_signal(barrier, inc=1, device_id={"tensor": flip(t, s)}, device_id_type=MESH)
    pl.semaphore_signal(barrier, inc=1, device_id={"dp": other_core}, device_id_type=MESH)
    pl.semaphore_wait(barrier, stages + 1)

    swap = pltpu.make_async_remote_copy(
        src_ref=att_ref,
        dst_ref=rows_all.at[pl.ds(rows, rows)],
        send_sem=pair_ssem.at[0],
        recv_sem=pair_rsem.at[0],
        device_id={"dp": other_core},
        device_id_type=MESH,
    )
    swap.start()
    rows_all[pl.ds(0, rows), :] = att_ref[...]

    def block_copy(x):
        return pltpu.make_async_remote_copy(
            src_ref=send_buf.at[x - 1],
            dst_ref=recv_buf.at[x - 1],
            send_sem=send_sem.at[x - 1],
            recv_sem=recv_sem.at[x - 1],
            device_id={"tensor": flip(t, low_stage(x))},
            device_id_type=MESH,
        )

    def step(x):
        load_w(x).wait()
        arrived = [x + (1 << s) for s in range(low_stage(x) if x else stages)]
        for a in arrived:
            block_copy(a).wait_recv()

        @pl.loop(0, width // tile)
        def _(j):
            cols = pl.ds(pl.multiple_of(j * tile, tile), tile)
            part = jnp.dot(
                att_ref[...], w_buf[x, :, cols], preferred_element_type=jnp.float32
            )
            for a in arrived:
                part = part + recv_buf[a - 1, :, cols].astype(jnp.float32)
            if x:
                send_buf[x - 1, :, cols] = part.astype(jnp.bfloat16)
            else:
                part = part + delta[pl.ds(0, rows), cols]
                part = part + delta_recv[:, cols].astype(jnp.float32)
                out_ref[:, cols] = part.astype(jnp.bfloat16)

        if x:
            block_copy(x).start()

    def low_copy(s):
        return pltpu.make_async_remote_copy(
            src_ref=low_send.at[s],
            dst_ref=low_recv.at[s],
            send_sem=low_ssem.at[s],
            recv_sem=low_rsem.at[s],
            device_id={"tensor": flip(t, s)},
            device_id_type=MESH,
        )

    first_lanes = lax.broadcasted_iota(jnp.int32, (rows, 2 * half), 1) < half

    def down():
        swap.wait_recv()

        def body(i, acc):
            load_piece(down_hbm, down_buf, down_sem, i).wait()
            span = pl.ds(pl.multiple_of(i * piece, piece), piece)
            got = lax.dot_general(
                rows_all[...], down_buf[span, :], (((1,), (1,)), ((), ())),
                preferred_element_type=jnp.float32,
            )
            for q in range(piece // (2 * half)):
                mine = code_ref[...] == i * (piece // (2 * half)) + q
                acc = acc + jnp.where(mine, got[:, 2 * half * q : 2 * half * (q + 1)], 0.0)
            return acc

        acc = lax.fori_loop(0, pieces, body, jnp.zeros((2 * rows, 2 * half), jnp.float32))
        acc = acc + pltpu.roll(acc, half, 1)
        low_send[0] = jnp.where(first_lanes, acc[:rows], acc[rows:])
        low_copy(0).start()

    def low_step(s):
        low_copy(s).wait_recv()
        low_send[s + 1] = low_send[s] + low_recv[s]
        if s + 1 < stages:
            low_copy(s + 1).start()

    back = pltpu.make_async_remote_copy(
        src_ref=delta_send,
        dst_ref=delta_recv,
        send_sem=pair_ssem.at[1],
        recv_sem=pair_rsem.at[1],
        device_id={"dp": other_core},
        device_id_type=MESH,
    )

    def up():
        packed = low_send[stages].astype(jnp.bfloat16).astype(jnp.float32)
        turned = pltpu.roll(packed, half, 1)
        low = jnp.concatenate(
            [jnp.where(first_lanes, packed, turned), jnp.where(first_lanes, turned, packed)], axis=0
        )
        delta[...] = jnp.zeros_like(delta)

        @pl.loop(0, pieces)
        def _(i):
            load_piece(up_hbm, up_buf, up_sem, i).wait()
            span = pl.ds(pl.multiple_of(i * piece, piece), piece)
            wide = jnp.concatenate(
                [
                    jnp.where(code_ref[...] == i * (piece // (2 * half)) + q, low, 0.0).astype(
                        jnp.bfloat16
                    )
                    for q in range(piece // (2 * half))
                ],
                axis=1,
            )
            delta[...] += jnp.dot(wide, up_buf[span, :], preferred_element_type=jnp.float32)

        delta_send[...] = delta[pl.ds(rows, rows), :].astype(jnp.bfloat16)
        back.start()

    step(order[0])
    for x in order[4:]:
        load_w(x).start()
    for i in range(pieces):
        load_piece(up_hbm, up_buf, up_sem, i).start()
    down()
    done = 0
    for at, x in enumerate(order[1:]):
        if x == 0:
            while done < stages:
                low_step(done)
                done += 1
                if done == stages:
                    up()
            back.wait_recv()
        step(x)
        if at >= 1 and done < stages:
            low_step(done)
            done += 1
            if done == stages:
                up()

    for x in range(1, n):
        block_copy(x).wait_send()
    for s in range(stages):
        low_copy(s).wait_send()
    swap.wait_send()
    back.wait_send()


def on_device(
    n,
    query,
    step_key_value,
    cache,
    output_projection_weight,
    adapter_down_weight,
    adapter_up_weight,
    row_adapter_index,
    adapter_storage_slot,
):
    att = attend(query, step_key_value, cache)
    rows, depth = att.shape
    width = output_projection_weight.shape[1] // n
    adapter_total = adapter_storage_slot.shape[0]
    matches = row_adapter_index[:, None] == jnp.arange(adapter_total, dtype=jnp.int32)[None, :]
    slot_all = jnp.sum(jnp.where(matches, adapter_storage_slot[None, :], 0), axis=1)
    me = lax.axis_index("dp")
    slots_here = adapter_up_weight.shape[0]
    rank = adapter_up_weight.shape[1]
    slots = jnp.concatenate(
        [
            lax.dynamic_slice_in_dim(slot_all, me * rows, rows),
            lax.dynamic_slice_in_dim(slot_all, (1 - me) * rows, rows),
        ]
    )
    local = slots - me * slots_here
    held = (local >= 0) & (local < slots_here)
    lane_half = (jnp.arange(2 * rank, dtype=jnp.int32) // rank)[None, :]
    code = jnp.where(held[:, None] & (local[:, None] % 2 == lane_half), local[:, None] // 2, -1)
    down_rows = adapter_down_weight.transpose(1, 2, 0).reshape(-1, depth)
    up_rows = adapter_up_weight.reshape(-1, width)
    stages = n.bit_length() - 1
    wide = down_rows.shape[0]
    pieces = 8
    vmem = pl.BlockSpec(memory_space=pltpu.VMEM)
    hbm = pl.BlockSpec(memory_space=pl.ANY)
    bf16, f32 = jnp.bfloat16, jnp.float32
    dma = pltpu.SemaphoreType.DMA
    return pl.pallas_call(
        functools.partial(project, n),
        out_shape=jax.ShapeDtypeStruct((rows, width), bf16),
        in_specs=[vmem, vmem, hbm, hbm, hbm],
        out_specs=vmem,
        scratch_shapes=[
            pltpu.VMEM((n, depth, width), bf16),
            pltpu.VMEM((wide, depth), bf16),
            pltpu.VMEM((wide, width), bf16),
            pltpu.VMEM((2 * rows, depth), bf16),
            pltpu.VMEM((n - 1, rows, width), bf16),
            pltpu.VMEM((n - 1, rows, width), bf16),
            pltpu.VMEM((stages + 1, rows, 2 * rank), f32),
            pltpu.VMEM((stages, rows, 2 * rank), f32),
            pltpu.VMEM((2 * rows, width), f32),
            pltpu.VMEM((rows, width), bf16),
            pltpu.VMEM((rows, width), bf16),
            dma((n,)),
            dma((pieces,)),
            dma((pieces,)),
            dma((n - 1,)),
            dma((n - 1,)),
            dma((stages,)),
            dma((stages,)),
            dma((2,)),
            dma((2,)),
        ],
        compiler_params=pltpu.CompilerParams(
            collective_id=0, has_side_effects=True, vmem_limit_bytes=52 * 1024 * 1024
        ),
        cost_estimate=pl.CostEstimate(
            flops=2 * rows * depth * width * n + 8 * rows * wide * depth,
            bytes_accessed=2 * (depth * width * n + 2 * wide * depth),
            transcendentals=0,
        ),
    )(att, code, output_projection_weight, down_rows, up_rows)


def solution(mesh):
    in_specs = (
        P(("parts", "dp"), "tensor"),
        P(("parts", "dp"), "tensor", None),
        P(("parts", "dp"), None, "tensor", None),
        P("tensor", None),
        P("tensor", "dp", None),
        P("dp", None, "tensor"),
        P("parts"),
        P(),
    )
    out_specs = P(("parts", "dp"), "tensor")
    return jax.shard_map(
        functools.partial(on_device, mesh.shape["tensor"]),
        mesh=mesh,
        in_specs=in_specs,
        out_specs=out_specs,
        check_vma=False,
    )
```

```python
import functools
import math

import jax
import jax.numpy as jnp
from jax import lax
from jax.experimental import pallas as pl
from jax.experimental.pallas import tpu as pltpu
from jax.sharding import PartitionSpec as P

MESH = pl.DeviceIdType.MESH


PARTS = 2
UNROLL = 16


def flip(index, stage):
    step = 1 << stage
    bit = lax.rem(lax.div(index, step), 2)
    return index + step - 2 * step * bit


def low_stage(relative):
    return (relative & -relative).bit_length() - 1


def project(
    n, query_ref, step_ref, code_ref, cache_hbm, w_hbm, down_hbm, up_hbm, out_ref,
    cache_buf, heads_buf, step_buf, summed_buf, w_buf, down_buf, up_buf, rows_all, send_buf, recv_buf, low_send, low_recv,
    delta, delta_send, delta_recv,
    cache_sem, w_sem, down_sem, up_sem, send_sem, recv_sem, low_ssem, low_rsem, pair_ssem, pair_rsem,
):
    stages = n.bit_length() - 1
    t = lax.axis_index("tensor")
    other_core = 1 - lax.axis_index("dp")
    rows, width = out_ref.shape
    share = rows // PARTS
    head_width = step_ref.shape[1] // 2
    group = query_ref.shape[1] // head_width
    pieces, piece = down_sem.shape[0], down_buf.shape[0] // down_sem.shape[0]
    tile = min(width, 512)
    half = 64

    def load_w(x):
        block = t
        for s in range(stages):
            if (x >> s) & 1:
                block = flip(block, s)
        return pltpu.make_async_copy(
            w_hbm.at[:, pl.ds(pl.multiple_of(block * width, width), width)],
            w_buf.at[x],
            w_sem.at[x],
        )

    def load_piece(src, dst, sem, i):
        span = pl.ds(pl.multiple_of(i * piece, piece), piece)
        return pltpu.make_async_copy(src.at[span], dst.at[span], sem.at[i])

    def load_cache(i):
        span = pl.ds(pl.multiple_of(i * UNROLL, UNROLL), UNROLL)
        return pltpu.make_async_copy(cache_hbm.at[span], cache_buf.at[span], cache_sem.at[i])

    odd = list(range(n - 1, 0, -2))
    even = list(range(n - 2, -1, -2))
    order = [odd[0]]
    for i in range(len(even) - 1):
        order += [odd[i + 1], even[i]]
    order += [0]
    chunks = share // UNROLL

    for p in range(PARTS):
        for i in range(p * chunks, (p + 1) * chunks):
            load_cache(i).start()
        load_w(order[p]).start()
    for x in order[PARTS:5]:
        load_w(x).start()
    for i in range(pieces):
        load_piece(down_hbm, down_buf, down_sem, i).start()
    for x in order[5:]:
        load_w(x).start()
    for i in range(pieces):
        load_piece(up_hbm, up_buf, up_sem, i).start()

    barrier = pltpu.get_barrier_semaphore()
    for s in range(stages):
        pl.semaphore_signal(barrier, inc=1, device_id={"tensor": flip(t, s)}, device_id_type=MESH)
    pl.semaphore_signal(barrier, inc=1, device_id={"dp": other_core}, device_id_type=MESH)
    pl.semaphore_wait(barrier, stages + 1)

    step_buf[...] = step_ref[...].astype(jnp.float32)
    for g in range(group):
        heads_buf[:, g, :] = query_ref[:, g * head_width : (g + 1) * head_width].astype(jnp.float32)
    score_scale = 1.0 / math.sqrt(head_width)

    def swap(p):
        return pltpu.make_async_remote_copy(
            src_ref=rows_all.at[pl.ds(p * share, share)],
            dst_ref=rows_all.at[pl.ds(rows + p * share, share)],
            send_sem=pair_ssem.at[p],
            recv_sem=pair_rsem.at[p],
            device_id={"dp": other_core},
            device_id_type=MESH,
        )

    def attend(p):
        @pl.loop(p * chunks, (p + 1) * chunks)
        def _(i):
            load_cache(i).wait()
            for u in range(UNROLL):
                r = i * UNROLL + u
                heads = heads_buf[r]
                own = step_buf[pl.ds(r, 1), :]
                scores = lax.dot_general(
                    heads.astype(jnp.bfloat16), cache_buf[r, :, :head_width],
                    (((1,), (1,)), ((), ())), preferred_element_type=jnp.float32,
                ) * score_scale
                own_score = jnp.sum(heads * own[:, :head_width], axis=1, keepdims=True) * score_scale
                peak = jnp.maximum(jnp.max(scores, axis=1, keepdims=True), own_score)
                expos = jnp.exp(scores - peak)
                own_expo = jnp.exp(own_score - peak)
                total = jnp.sum(expos, axis=1, keepdims=True) + own_expo
                weights = (expos / total).astype(jnp.bfloat16)
                own_weight = (own_expo / total).astype(jnp.bfloat16).astype(jnp.float32)
                summed_buf[r] = (
                    jnp.dot(
                        weights, cache_buf[r, :, head_width:], preferred_element_type=jnp.float32
                    )
                    + own_weight * own[:, head_width:]
                )

        mine = pl.ds(p * share, share)
        for g in range(group):
            rows_all[mine, g * head_width : (g + 1) * head_width] = summed_buf[mine, g, :].astype(
                jnp.bfloat16
            )
        swap(p).start()

    def block_copy(x, p):
        span = pl.ds(p * share, share)
        return pltpu.make_async_remote_copy(
            src_ref=send_buf.at[x - 1, span],
            dst_ref=recv_buf.at[x - 1, span],
            send_sem=send_sem.at[x - 1, p],
            recv_sem=recv_sem.at[x - 1, p],
            device_id={"tensor": flip(t, low_stage(x))},
            device_id_type=MESH,
        )

    def step(x, p):
        if p == 0:
            load_w(x).wait()
        span = pl.ds(p * share, share)
        arrived = [x + (1 << s) for s in range(low_stage(x) if x else stages)]
        for a in arrived:
            block_copy(a, p).wait_recv()

        @pl.loop(0, width // tile)
        def _(j):
            cols = pl.ds(pl.multiple_of(j * tile, tile), tile)
            part = jnp.dot(
                rows_all[span, :], w_buf[x, :, cols], preferred_element_type=jnp.float32
            )
            for a in arrived:
                part = part + recv_buf[a - 1, span, cols].astype(jnp.float32)
            if x:
                send_buf[x - 1, span, cols] = part.astype(jnp.bfloat16)
            else:
                part = part + delta[span, cols]
                part = part + delta_recv[span, cols].astype(jnp.float32)
                out_ref[span, cols] = part.astype(jnp.bfloat16)

        if x:
            block_copy(x, p).start()

    def low_copy(s):
        return pltpu.make_async_remote_copy(
            src_ref=low_send.at[s],
            dst_ref=low_recv.at[s],
            send_sem=low_ssem.at[s],
            recv_sem=low_rsem.at[s],
            device_id={"tensor": flip(t, s)},
            device_id_type=MESH,
        )

    first_lanes = lax.broadcasted_iota(jnp.int32, (rows, 2 * half), 1) < half

    def down():
        for p in range(PARTS):
            swap(p).wait_recv()

        def body(i, acc):
            load_piece(down_hbm, down_buf, down_sem, i).wait()
            span = pl.ds(pl.multiple_of(i * piece, piece), piece)
            got = lax.dot_general(
                rows_all[...], down_buf[span, :], (((1,), (1,)), ((), ())),
                preferred_element_type=jnp.float32,
            )
            for q in range(piece // (2 * half)):
                mine = code_ref[...] == i * (piece // (2 * half)) + q
                acc = acc + jnp.where(mine, got[:, 2 * half * q : 2 * half * (q + 1)], 0.0)
            return acc

        acc = lax.fori_loop(0, pieces, body, jnp.zeros((2 * rows, 2 * half), jnp.float32))
        acc = acc + pltpu.roll(acc, half, 1)
        low_send[0] = jnp.where(first_lanes, acc[:rows], acc[rows:])
        low_copy(0).start()

    def low_step(s):
        low_copy(s).wait_recv()
        low_send[s + 1] = low_send[s] + low_recv[s]
        if s + 1 < stages:
            low_copy(s + 1).start()

    back = pltpu.make_async_remote_copy(
        src_ref=delta_send,
        dst_ref=delta_recv,
        send_sem=pair_ssem.at[PARTS],
        recv_sem=pair_rsem.at[PARTS],
        device_id={"dp": other_core},
        device_id_type=MESH,
    )

    def up():
        packed = low_send[stages].astype(jnp.bfloat16).astype(jnp.float32)
        turned = pltpu.roll(packed, half, 1)
        low = jnp.concatenate(
            [jnp.where(first_lanes, packed, turned), jnp.where(first_lanes, turned, packed)], axis=0
        )
        delta[...] = jnp.zeros_like(delta)

        @pl.loop(0, pieces)
        def _(i):
            load_piece(up_hbm, up_buf, up_sem, i).wait()
            span = pl.ds(pl.multiple_of(i * piece, piece), piece)
            wide = jnp.concatenate(
                [
                    jnp.where(code_ref[...] == i * (piece // (2 * half)) + q, low, 0.0).astype(
                        jnp.bfloat16
                    )
                    for q in range(piece // (2 * half))
                ],
                axis=1,
            )
            delta[...] += jnp.dot(wide, up_buf[span, :], preferred_element_type=jnp.float32)

        delta_send[...] = delta[pl.ds(rows, rows), :].astype(jnp.bfloat16)
        back.start()

    attend(0)
    step(order[0], 0)
    step(order[1], 0)
    attend(1)
    step(order[0], 1)
    down()
    done = 0
    for at in range(1, n):
        if order[at] == 0:
            while done < stages:
                low_step(done)
                done += 1
                if done == stages:
                    up()
            back.wait_recv()
        if at >= 2:
            step(order[at], 0)
        step(order[at], 1)
        if at >= 2 and done < stages:
            low_step(done)
            done += 1
            if done == stages:
                up()

    for x in range(1, n):
        for p in range(PARTS):
            block_copy(x, p).wait_send()
    for s in range(stages):
        low_copy(s).wait_send()
    for p in range(PARTS):
        swap(p).wait_send()
    back.wait_send()


def on_device(
    n,
    query,
    step_key_value,
    cache,
    output_projection_weight,
    adapter_down_weight,
    adapter_up_weight,
    row_adapter_index,
    adapter_storage_slot,
):
    rows, depth = query.shape
    context, both = cache.shape[1], cache.shape[3]
    head_width = both // 2
    width = output_projection_weight.shape[1] // n
    adapter_total = adapter_storage_slot.shape[0]
    matches = row_adapter_index[:, None] == jnp.arange(adapter_total, dtype=jnp.int32)[None, :]
    slot_all = jnp.sum(jnp.where(matches, adapter_storage_slot[None, :], 0), axis=1)
    me = lax.axis_index("dp")
    slots_here = adapter_up_weight.shape[0]
    rank = adapter_up_weight.shape[1]
    slots = jnp.concatenate(
        [
            lax.dynamic_slice_in_dim(slot_all, me * rows, rows),
            lax.dynamic_slice_in_dim(slot_all, (1 - me) * rows, rows),
        ]
    )
    local = slots - me * slots_here
    held = (local >= 0) & (local < slots_here)
    lane_half = (jnp.arange(2 * rank, dtype=jnp.int32) // rank)[None, :]
    code = jnp.where(held[:, None] & (local[:, None] % 2 == lane_half), local[:, None] // 2, -1)
    down_rows = adapter_down_weight.transpose(1, 2, 0).reshape(-1, depth)
    up_rows = adapter_up_weight.reshape(-1, width)
    stages = n.bit_length() - 1
    wide = down_rows.shape[0]
    pieces = 8
    vmem = pl.BlockSpec(memory_space=pltpu.VMEM)
    hbm = pl.BlockSpec(memory_space=pl.ANY)
    bf16, f32 = jnp.bfloat16, jnp.float32
    dma = pltpu.SemaphoreType.DMA
    return pl.pallas_call(
        functools.partial(project, n),
        out_shape=jax.ShapeDtypeStruct((rows, width), bf16),
        in_specs=[vmem, vmem, vmem, hbm, hbm, hbm, hbm],
        out_specs=vmem,
        scratch_shapes=[
            pltpu.VMEM((rows, context, both), bf16),
            pltpu.VMEM((rows, depth // head_width, head_width), f32),
            pltpu.VMEM((rows, both), f32),
            pltpu.VMEM((rows, depth // head_width, head_width), f32),
            pltpu.VMEM((n, depth, width), bf16),
            pltpu.VMEM((wide, depth), bf16),
            pltpu.VMEM((wide, width), bf16),
            pltpu.VMEM((2 * rows, depth), bf16),
            pltpu.VMEM((n - 1, rows, width), bf16),
            pltpu.VMEM((n - 1, rows, width), bf16),
            pltpu.VMEM((stages + 1, rows, 2 * rank), f32),
            pltpu.VMEM((stages, rows, 2 * rank), f32),
            pltpu.VMEM((2 * rows, width), f32),
            pltpu.VMEM((rows, width), bf16),
            pltpu.VMEM((rows, width), bf16),
            dma((rows // UNROLL,)),
            dma((n,)),
            dma((pieces,)),
            dma((pieces,)),
            dma((n - 1, PARTS)),
            dma((n - 1, PARTS)),
            dma((stages,)),
            dma((stages,)),
            dma((PARTS + 1,)),
            dma((PARTS + 1,)),
        ],
        compiler_params=pltpu.CompilerParams(
            collective_id=0, has_side_effects=True, vmem_limit_bytes=56 * 1024 * 1024
        ),
        cost_estimate=pl.CostEstimate(
            flops=2 * rows * depth * width * n + 8 * rows * wide * depth,
            bytes_accessed=2 * (depth * width * n + 2 * wide * depth),
            transcendentals=0,
        ),
    )(
        query, step_key_value.reshape(rows, both), code, cache.reshape(rows, context, both),
        output_projection_weight, down_rows, up_rows,
    )


def solution(mesh):
    in_specs = (
        P(("parts", "dp"), "tensor"),
        P(("parts", "dp"), "tensor", None),
        P(("parts", "dp"), None, "tensor", None),
        P("tensor", None),
        P("tensor", "dp", None),
        P("dp", None, "tensor"),
        P("parts"),
        P(),
    )
    out_specs = P(("parts", "dp"), "tensor")
    return jax.shard_map(
        functools.partial(on_device, mesh.shape["tensor"]),
        mesh=mesh,
        in_specs=in_specs,
        out_specs=out_specs,
        check_vma=False,
    )
```

```python
import functools
import math

import jax
import jax.numpy as jnp
from jax import lax
from jax.experimental import pallas as pl
from jax.experimental.pallas import tpu as pltpu
from jax.sharding import PartitionSpec as P

MESH = pl.DeviceIdType.MESH


PARTS = 2


def attend(query, step_key_value, cache):
    row_count = query.shape[0]
    copies = cache.shape[2]
    head_width = cache.shape[3] // 2
    group = query.shape[1] // (copies * head_width)
    heads = query.reshape(row_count, copies, group, head_width)
    score_scale = 1.0 / math.sqrt(head_width)
    scores = (
        jnp.einsum(
            "rsgd,rcsd->rsgc", heads, cache[..., :head_width], preferred_element_type=jnp.float32
        )
        * score_scale
    )
    own_score = (
        jnp.einsum(
            "rsgd,rsd->rsg",
            heads,
            step_key_value[..., :head_width],
            preferred_element_type=jnp.float32,
        )
        * score_scale
    )
    peak = jnp.maximum(jnp.max(scores, axis=-1), own_score)
    expos = jnp.exp(scores - peak[..., None])
    own_expo = jnp.exp(own_score - peak)
    total = jnp.sum(expos, axis=-1) + own_expo
    weights = (expos / total[..., None]).astype(jnp.bfloat16)
    own_weight = (own_expo / total).astype(jnp.bfloat16)
    summed = jnp.einsum(
        "rsgc,rcsd->rsgd", weights, cache[..., head_width:], preferred_element_type=jnp.float32
    )
    summed = summed + own_weight.astype(jnp.float32)[..., None] * step_key_value[
        :, :, None, head_width:
    ].astype(jnp.float32)
    return summed.astype(jnp.bfloat16).reshape(row_count, -1)


def flip(index, stage):
    step = 1 << stage
    bit = lax.rem(lax.div(index, step), 2)
    return index + step - 2 * step * bit


def low_stage(relative):
    return (relative & -relative).bit_length() - 1


def project(
    n, att_ref, code_ref, w_hbm, down_hbm, up_hbm, out_ref,
    w_buf, down_buf, up_buf, rows_all, send_buf, recv_buf, low_send, low_recv,
    delta, delta_send, delta_recv,
    w_sem, down_sem, up_sem, send_sem, recv_sem, low_ssem, low_rsem, pair_ssem, pair_rsem,
):
    stages = n.bit_length() - 1
    t = lax.axis_index("tensor")
    other_core = 1 - lax.axis_index("dp")
    rows, width = out_ref.shape
    share = rows // PARTS
    pieces, piece = down_sem.shape[0], down_buf.shape[0] // down_sem.shape[0]
    tile = min(width, 512)
    half = 64

    def load_w(x):
        block = t
        for s in range(stages):
            if (x >> s) & 1:
                block = flip(block, s)
        return pltpu.make_async_copy(
            w_hbm.at[:, pl.ds(pl.multiple_of(block * width, width), width)],
            w_buf.at[x],
            w_sem.at[x],
        )

    def load_piece(src, dst, sem, i):
        span = pl.ds(pl.multiple_of(i * piece, piece), piece)
        return pltpu.make_async_copy(src.at[span], dst.at[span], sem.at[i])

    def real_stage(s, p):
        return 1 - s if p == PARTS - 1 and s < 2 else s

    def real(x, p):
        return sum(((x >> s) & 1) << real_stage(s, p) for s in range(stages))

    loaded = set()
    odd = list(range(n - 1, 0, -2))
    even = list(range(n - 2, -1, -2))
    first = []
    for x in odd + even:
        for p in range(PARTS):
            if real(x, p) not in first:
                first.append(real(x, p))
    for x in first[:3]:
        load_w(x).start()
    for i in range(pieces):
        load_piece(down_hbm, down_buf, down_sem, i).start()
    for x in first[3:]:
        load_w(x).start()
    for i in range(pieces):
        load_piece(up_hbm, up_buf, up_sem, i).start()

    barrier = pltpu.get_barrier_semaphore()
    for s in range(stages):
        pl.semaphore_signal(barrier, inc=1, device_id={"tensor": flip(t, s)}, device_id_type=MESH)
    pl.semaphore_signal(barrier, inc=1, device_id={"dp": other_core}, device_id_type=MESH)
    pl.semaphore_wait(barrier, stages + 1)

    def swap(p):
        return pltpu.make_async_remote_copy(
            src_ref=att_ref.at[pl.ds(p * share, share)],
            dst_ref=rows_all.at[pl.ds(rows + p * share, share)],
            send_sem=pair_ssem.at[p],
            recv_sem=pair_rsem.at[p],
            device_id={"dp": other_core},
            device_id_type=MESH,
        )

    def block_copy(x, p):
        span = pl.ds(p * share, share)
        return pltpu.make_async_remote_copy(
            src_ref=send_buf.at[x - 1, span],
            dst_ref=recv_buf.at[x - 1, span],
            send_sem=send_sem.at[x - 1, p],
            recv_sem=recv_sem.at[x - 1, p],
            device_id={"tensor": flip(t, real_stage(low_stage(x), p))},
            device_id_type=MESH,
        )

    def step(x, p):
        held = real(x, p)
        if held not in loaded:
            loaded.add(held)
            load_w(held).wait()
        span = pl.ds(p * share, share)
        arrived = [x + (1 << s) for s in range(low_stage(x) if x else stages)]
        for a in arrived:
            block_copy(a, p).wait_recv()

        @pl.loop(0, width // tile)
        def _(j):
            cols = pl.ds(pl.multiple_of(j * tile, tile), tile)
            part = jnp.dot(
                rows_all[span, :], w_buf[held, :, cols], preferred_element_type=jnp.float32
            )
            for a in arrived:
                part = part + recv_buf[a - 1, span, cols].astype(jnp.float32)
            if x:
                send_buf[x - 1, span, cols] = part.astype(jnp.bfloat16)
            else:
                part = part + delta[span, cols]
                part = part + delta_recv[span, cols].astype(jnp.float32)
                out_ref[span, cols] = part.astype(jnp.bfloat16)

        if x:
            block_copy(x, p).start()

    def low_copy(s):
        return pltpu.make_async_remote_copy(
            src_ref=low_send.at[s],
            dst_ref=low_recv.at[s],
            send_sem=low_ssem.at[s],
            recv_sem=low_rsem.at[s],
            device_id={"tensor": flip(t, s)},
            device_id_type=MESH,
        )

    first_lanes = lax.broadcasted_iota(jnp.int32, (rows, 2 * half), 1) < half

    def down():
        for p in range(PARTS):
            swap(p).wait_recv()

        def body(i, acc):
            load_piece(down_hbm, down_buf, down_sem, i).wait()
            span = pl.ds(pl.multiple_of(i * piece, piece), piece)
            got = lax.dot_general(
                rows_all[...], down_buf[span, :], (((1,), (1,)), ((), ())),
                preferred_element_type=jnp.float32,
            )
            for q in range(piece // (2 * half)):
                mine = code_ref[...] == i * (piece // (2 * half)) + q
                acc = acc + jnp.where(mine, got[:, 2 * half * q : 2 * half * (q + 1)], 0.0)
            return acc

        acc = lax.fori_loop(0, pieces, body, jnp.zeros((2 * rows, 2 * half), jnp.float32))
        acc = acc + pltpu.roll(acc, half, 1)
        low_send[0] = jnp.where(first_lanes, acc[:rows], acc[rows:])
        low_copy(0).start()

    def low_step(s):
        low_copy(s).wait_recv()
        low_send[s + 1] = low_send[s] + low_recv[s]
        if s + 1 < stages:
            low_copy(s + 1).start()

    back = pltpu.make_async_remote_copy(
        src_ref=delta_send,
        dst_ref=delta_recv,
        send_sem=pair_ssem.at[PARTS],
        recv_sem=pair_rsem.at[PARTS],
        device_id={"dp": other_core},
        device_id_type=MESH,
    )

    def up():
        packed = low_send[stages].astype(jnp.bfloat16).astype(jnp.float32)
        turned = pltpu.roll(packed, half, 1)
        low = jnp.concatenate(
            [jnp.where(first_lanes, packed, turned), jnp.where(first_lanes, turned, packed)], axis=0
        )
        delta[...] = jnp.zeros_like(delta)

        @pl.loop(0, pieces)
        def _(i):
            load_piece(up_hbm, up_buf, up_sem, i).wait()
            span = pl.ds(pl.multiple_of(i * piece, piece), piece)
            wide = jnp.concatenate(
                [
                    jnp.where(code_ref[...] == i * (piece // (2 * half)) + q, low, 0.0).astype(
                        jnp.bfloat16
                    )
                    for q in range(piece // (2 * half))
                ],
                axis=1,
            )
            delta[...] += jnp.dot(wide, up_buf[span, :], preferred_element_type=jnp.float32)

        delta_send[...] = delta[pl.ds(rows, rows), :].astype(jnp.bfloat16)
        back.start()

    for p in range(PARTS):
        swap(p).start()
    rows_all[pl.ds(0, rows), :] = att_ref[...]
    for x in odd[:2]:
        for p in range(PARTS):
            step(x, p)
    down()
    for p in range(PARTS):
        step(odd[2], p)
        step(even[0], p)
    for x in odd[3:]:
        for p in range(PARTS):
            step(x, p)
    done = 0
    for x in even[1:-1]:
        if done < stages - 1:
            low_step(done)
            done += 1
        for p in range(PARTS):
            step(x, p)
    while done < stages:
        low_step(done)
        done += 1
    up()
    back.wait_recv()
    for p in range(PARTS):
        step(0, p)

    for x in range(1, n):
        for p in range(PARTS):
            block_copy(x, p).wait_send()
    for s in range(stages):
        low_copy(s).wait_send()
    for p in range(PARTS):
        swap(p).wait_send()
    back.wait_send()


def on_device(
    n,
    query,
    step_key_value,
    cache,
    output_projection_weight,
    adapter_down_weight,
    adapter_up_weight,
    row_adapter_index,
    adapter_storage_slot,
):
    att = attend(query, step_key_value, cache)
    rows, depth = att.shape
    width = output_projection_weight.shape[1] // n
    adapter_total = adapter_storage_slot.shape[0]
    matches = row_adapter_index[:, None] == jnp.arange(adapter_total, dtype=jnp.int32)[None, :]
    slot_all = jnp.sum(jnp.where(matches, adapter_storage_slot[None, :], 0), axis=1)
    me = lax.axis_index("dp")
    slots_here = adapter_up_weight.shape[0]
    rank = adapter_up_weight.shape[1]
    slots = jnp.concatenate(
        [
            lax.dynamic_slice_in_dim(slot_all, me * rows, rows),
            lax.dynamic_slice_in_dim(slot_all, (1 - me) * rows, rows),
        ]
    )
    local = slots - me * slots_here
    held = (local >= 0) & (local < slots_here)
    lane_half = (jnp.arange(2 * rank, dtype=jnp.int32) // rank)[None, :]
    code = jnp.where(held[:, None] & (local[:, None] % 2 == lane_half), local[:, None] // 2, -1)
    down_rows = adapter_down_weight.transpose(1, 2, 0).reshape(-1, depth)
    up_rows = adapter_up_weight.reshape(-1, width)
    stages = n.bit_length() - 1
    wide = down_rows.shape[0]
    pieces = 8
    vmem = pl.BlockSpec(memory_space=pltpu.VMEM)
    hbm = pl.BlockSpec(memory_space=pl.ANY)
    bf16, f32 = jnp.bfloat16, jnp.float32
    dma = pltpu.SemaphoreType.DMA
    return pl.pallas_call(
        functools.partial(project, n),
        out_shape=jax.ShapeDtypeStruct((rows, width), bf16),
        in_specs=[vmem, vmem, hbm, hbm, hbm],
        out_specs=vmem,
        scratch_shapes=[
            pltpu.VMEM((n, depth, width), bf16),
            pltpu.VMEM((wide, depth), bf16),
            pltpu.VMEM((wide, width), bf16),
            pltpu.VMEM((2 * rows, depth), bf16),
            pltpu.VMEM((n - 1, rows, width), bf16),
            pltpu.VMEM((n - 1, rows, width), bf16),
            pltpu.VMEM((stages + 1, rows, 2 * rank), f32),
            pltpu.VMEM((stages, rows, 2 * rank), f32),
            pltpu.VMEM((2 * rows, width), f32),
            pltpu.VMEM((rows, width), bf16),
            pltpu.VMEM((rows, width), bf16),
            dma((n,)),
            dma((pieces,)),
            dma((pieces,)),
            dma((n - 1, PARTS)),
            dma((n - 1, PARTS)),
            dma((stages,)),
            dma((stages,)),
            dma((PARTS + 1,)),
            dma((PARTS + 1,)),
        ],
        compiler_params=pltpu.CompilerParams(
            collective_id=0, has_side_effects=True, vmem_limit_bytes=52 * 1024 * 1024
        ),
        cost_estimate=pl.CostEstimate(
            flops=2 * rows * depth * width * n + 8 * rows * wide * depth,
            bytes_accessed=2 * (depth * width * n + 2 * wide * depth),
            transcendentals=0,
        ),
    )(
        att, code, output_projection_weight, down_rows, up_rows,
    )


def solution(mesh):
    in_specs = (
        P(("parts", "dp"), "tensor"),
        P(("parts", "dp"), "tensor", None),
        P(("parts", "dp"), None, "tensor", None),
        P("tensor", None),
        P("tensor", "dp", None),
        P("dp", None, "tensor"),
        P("parts"),
        P(),
    )
    out_specs = P(("parts", "dp"), "tensor")
    return jax.shard_map(
        functools.partial(on_device, mesh.shape["tensor"]),
        mesh=mesh,
        in_specs=in_specs,
        out_specs=out_specs,
        check_vma=False,
    )
```

```python
import functools
import math

import jax
import jax.numpy as jnp
from jax import lax
from jax.experimental import pallas as pl
from jax.experimental.pallas import tpu as pltpu
from jax.sharding import PartitionSpec as P

MESH = pl.DeviceIdType.MESH


PARTS = 2


def attend(query, step_key_value, cache):
    row_count = query.shape[0]
    copies = cache.shape[2]
    head_width = cache.shape[3] // 2
    group = query.shape[1] // (copies * head_width)
    heads = query.reshape(row_count, copies, group, head_width)
    score_scale = 1.0 / math.sqrt(head_width)
    scores = (
        jnp.einsum(
            "rsgd,rcsd->rsgc", heads, cache[..., :head_width], preferred_element_type=jnp.float32
        )
        * score_scale
    )
    own_score = (
        jnp.einsum(
            "rsgd,rsd->rsg",
            heads,
            step_key_value[..., :head_width],
            preferred_element_type=jnp.float32,
        )
        * score_scale
    )
    peak = jnp.maximum(jnp.max(scores, axis=-1), own_score)
    expos = jnp.exp(scores - peak[..., None])
    own_expo = jnp.exp(own_score - peak)
    total = jnp.sum(expos, axis=-1) + own_expo
    weights = (expos / total[..., None]).astype(jnp.bfloat16)
    own_weight = (own_expo / total).astype(jnp.bfloat16)
    summed = jnp.einsum(
        "rsgc,rcsd->rsgd", weights, cache[..., head_width:], preferred_element_type=jnp.float32
    )
    summed = summed + own_weight.astype(jnp.float32)[..., None] * step_key_value[
        :, :, None, head_width:
    ].astype(jnp.float32)
    return summed.astype(jnp.bfloat16).reshape(row_count, -1)


def flip(index, stage):
    step = 1 << stage
    bit = lax.rem(lax.div(index, step), 2)
    return index + step - 2 * step * bit


def low_stage(relative):
    return (relative & -relative).bit_length() - 1


def project(
    n, att_ref, code_ref, w_hbm, down_hbm, up_hbm, out_ref,
    w_buf, down_buf, up_buf, rows_all, send_buf, recv_buf, low_send, low_recv,
    delta, delta_send, delta_recv,
    w_sem, down_sem, up_sem, send_sem, recv_sem, low_ssem, low_rsem, pair_ssem, pair_rsem,
):
    stages = n.bit_length() - 1
    t = lax.axis_index("tensor")
    other_core = 1 - lax.axis_index("dp")
    rows, width = out_ref.shape
    share = rows // PARTS
    pieces, piece = down_sem.shape[0], down_buf.shape[0] // down_sem.shape[0]
    tile = min(width, 512)
    half = 64

    def load_w(x):
        block = t
        for s in range(stages):
            if (x >> s) & 1:
                block = flip(block, s)
        return pltpu.make_async_copy(
            w_hbm.at[:, pl.ds(pl.multiple_of(block * width, width), width)],
            w_buf.at[x],
            w_sem.at[x],
        )

    def load_piece(src, dst, sem, i):
        span = pl.ds(pl.multiple_of(i * piece, piece), piece)
        return pltpu.make_async_copy(src.at[span], dst.at[span], sem.at[i])

    def real_stage(s, p):
        return 1 - s if p == PARTS - 1 and s < 2 else s

    def real(x, p):
        return sum(((x >> s) & 1) << real_stage(s, p) for s in range(stages))

    loaded = set()
    odd = list(range(n - 1, 0, -2))
    even = list(range(n - 2, -1, -2))
    first = []
    for x in odd + even:
        for p in range(PARTS):
            if real(x, p) not in first:
                first.append(real(x, p))
    for x in first[: n // 2 + 1]:
        load_w(x).start()
    for i in range(pieces):
        load_piece(down_hbm, down_buf, down_sem, i).start()
    for x in first[n // 2 + 1 :]:
        load_w(x).start()
    for i in range(pieces):
        load_piece(up_hbm, up_buf, up_sem, i).start()

    barrier = pltpu.get_barrier_semaphore()
    for s in range(stages):
        pl.semaphore_signal(barrier, inc=1, device_id={"tensor": flip(t, s)}, device_id_type=MESH)
    pl.semaphore_signal(barrier, inc=1, device_id={"dp": other_core}, device_id_type=MESH)
    pl.semaphore_wait(barrier, stages + 1)

    def swap(p):
        return pltpu.make_async_remote_copy(
            src_ref=att_ref.at[pl.ds(p * share, share)],
            dst_ref=rows_all.at[pl.ds(rows + p * share, share)],
            send_sem=pair_ssem.at[p],
            recv_sem=pair_rsem.at[p],
            device_id={"dp": other_core},
            device_id_type=MESH,
        )

    def block_copy(x, p):
        span = pl.ds(p * share, share)
        return pltpu.make_async_remote_copy(
            src_ref=send_buf.at[x - 1, span],
            dst_ref=recv_buf.at[x - 1, span],
            send_sem=send_sem.at[x - 1, p],
            recv_sem=recv_sem.at[x - 1, p],
            device_id={"tensor": flip(t, real_stage(low_stage(x), p))},
            device_id_type=MESH,
        )

    def step(x, p):
        held = real(x, p)
        if held not in loaded:
            loaded.add(held)
            load_w(held).wait()
        span = pl.ds(p * share, share)
        arrived = [x + (1 << s) for s in range(low_stage(x) if x else stages)]
        for a in arrived:
            block_copy(a, p).wait_recv()

        @pl.loop(0, width // tile)
        def _(j):
            cols = pl.ds(pl.multiple_of(j * tile, tile), tile)
            part = jnp.dot(
                rows_all[span, :], w_buf[held, :, cols], preferred_element_type=jnp.float32
            )
            for a in arrived:
                part = part + recv_buf[a - 1, span, cols].astype(jnp.float32)
            if x:
                send_buf[x - 1, span, cols] = part.astype(jnp.bfloat16)
            else:
                part = part + delta[span, cols]
                part = part + delta_recv[span, cols].astype(jnp.float32)
                out_ref[span, cols] = part.astype(jnp.bfloat16)

        if x:
            block_copy(x, p).start()

    def low_copy(s):
        return pltpu.make_async_remote_copy(
            src_ref=low_send.at[s],
            dst_ref=low_recv.at[s],
            send_sem=low_ssem.at[s],
            recv_sem=low_rsem.at[s],
            device_id={"tensor": flip(t, s)},
            device_id_type=MESH,
        )

    first_lanes = lax.broadcasted_iota(jnp.int32, (rows, 2 * half), 1) < half

    def down():
        for p in range(PARTS):
            swap(p).wait_recv()

        def body(i, acc):
            load_piece(down_hbm, down_buf, down_sem, i).wait()
            span = pl.ds(pl.multiple_of(i * piece, piece), piece)
            got = lax.dot_general(
                rows_all[...], down_buf[span, :], (((1,), (1,)), ((), ())),
                preferred_element_type=jnp.float32,
            )
            for q in range(piece // (2 * half)):
                mine = code_ref[...] == i * (piece // (2 * half)) + q
                acc = acc + jnp.where(mine, got[:, 2 * half * q : 2 * half * (q + 1)], 0.0)
            return acc

        acc = lax.fori_loop(0, pieces, body, jnp.zeros((2 * rows, 2 * half), jnp.float32))
        acc = acc + pltpu.roll(acc, half, 1)
        low_send[0] = jnp.where(first_lanes, acc[:rows], acc[rows:])
        low_copy(0).start()

    def low_step(s):
        low_copy(s).wait_recv()
        low_send[s + 1] = low_send[s] + low_recv[s]
        if s + 1 < stages:
            low_copy(s + 1).start()

    back = pltpu.make_async_remote_copy(
        src_ref=delta_send,
        dst_ref=delta_recv,
        send_sem=pair_ssem.at[PARTS],
        recv_sem=pair_rsem.at[PARTS],
        device_id={"dp": other_core},
        device_id_type=MESH,
    )

    def up():
        packed = low_send[stages].astype(jnp.bfloat16).astype(jnp.float32)
        turned = pltpu.roll(packed, half, 1)
        low = jnp.concatenate(
            [jnp.where(first_lanes, packed, turned), jnp.where(first_lanes, turned, packed)], axis=0
        )
        delta[...] = jnp.zeros_like(delta)

        @pl.loop(0, pieces)
        def _(i):
            load_piece(up_hbm, up_buf, up_sem, i).wait()
            span = pl.ds(pl.multiple_of(i * piece, piece), piece)
            wide = jnp.concatenate(
                [
                    jnp.where(code_ref[...] == i * (piece // (2 * half)) + q, low, 0.0).astype(
                        jnp.bfloat16
                    )
                    for q in range(piece // (2 * half))
                ],
                axis=1,
            )
            delta[...] += jnp.dot(wide, up_buf[span, :], preferred_element_type=jnp.float32)

        delta_send[...] = delta[pl.ds(rows, rows), :].astype(jnp.bfloat16)
        back.start()

    for p in range(PARTS):
        swap(p).start()
    rows_all[pl.ds(0, rows), :] = att_ref[...]
    for x in odd:
        for p in range(PARTS):
            step(x, p)
    down()
    for p in range(PARTS):
        step(even[0], p)
    done = 0
    for x in even[1:-1]:
        if done < stages - 1:
            low_step(done)
            done += 1
        for p in range(PARTS):
            step(x, p)
    while done < stages:
        low_step(done)
        done += 1
    up()
    back.wait_recv()
    for p in range(PARTS):
        step(0, p)

    for x in range(1, n):
        for p in range(PARTS):
            block_copy(x, p).wait_send()
    for s in range(stages):
        low_copy(s).wait_send()
    for p in range(PARTS):
        swap(p).wait_send()
    back.wait_send()


def on_device(
    n,
    query,
    step_key_value,
    cache,
    output_projection_weight,
    adapter_down_weight,
    adapter_up_weight,
    row_adapter_index,
    adapter_storage_slot,
):
    att = attend(query, step_key_value, cache)
    rows, depth = att.shape
    width = output_projection_weight.shape[1] // n
    adapter_total = adapter_storage_slot.shape[0]
    matches = row_adapter_index[:, None] == jnp.arange(adapter_total, dtype=jnp.int32)[None, :]
    slot_all = jnp.sum(jnp.where(matches, adapter_storage_slot[None, :], 0), axis=1)
    me = lax.axis_index("dp")
    slots_here = adapter_up_weight.shape[0]
    rank = adapter_up_weight.shape[1]
    slots = jnp.concatenate(
        [
            lax.dynamic_slice_in_dim(slot_all, me * rows, rows),
            lax.dynamic_slice_in_dim(slot_all, (1 - me) * rows, rows),
        ]
    )
    local = slots - me * slots_here
    held = (local >= 0) & (local < slots_here)
    lane_half = (jnp.arange(2 * rank, dtype=jnp.int32) // rank)[None, :]
    code = jnp.where(held[:, None] & (local[:, None] % 2 == lane_half), local[:, None] // 2, -1)
    down_rows = adapter_down_weight.transpose(1, 2, 0).reshape(-1, depth)
    up_rows = adapter_up_weight.reshape(-1, width)
    stages = n.bit_length() - 1
    wide = down_rows.shape[0]
    pieces = 8
    vmem = pl.BlockSpec(memory_space=pltpu.VMEM)
    hbm = pl.BlockSpec(memory_space=pl.ANY)
    bf16, f32 = jnp.bfloat16, jnp.float32
    dma = pltpu.SemaphoreType.DMA
    return pl.pallas_call(
        functools.partial(project, n),
        out_shape=jax.ShapeDtypeStruct((rows, width), bf16),
        in_specs=[vmem, vmem, hbm, hbm, hbm],
        out_specs=vmem,
        scratch_shapes=[
            pltpu.VMEM((n, depth, width), bf16),
            pltpu.VMEM((wide, depth), bf16),
            pltpu.VMEM((wide, width), bf16),
            pltpu.VMEM((2 * rows, depth), bf16),
            pltpu.VMEM((n - 1, rows, width), bf16),
            pltpu.VMEM((n - 1, rows, width), bf16),
            pltpu.VMEM((stages + 1, rows, 2 * rank), f32),
            pltpu.VMEM((stages, rows, 2 * rank), f32),
            pltpu.VMEM((2 * rows, width), f32),
            pltpu.VMEM((rows, width), bf16),
            pltpu.VMEM((rows, width), bf16),
            dma((n,)),
            dma((pieces,)),
            dma((pieces,)),
            dma((n - 1, PARTS)),
            dma((n - 1, PARTS)),
            dma((stages,)),
            dma((stages,)),
            dma((PARTS + 1,)),
            dma((PARTS + 1,)),
        ],
        compiler_params=pltpu.CompilerParams(
            collective_id=0, has_side_effects=True, vmem_limit_bytes=52 * 1024 * 1024
        ),
        cost_estimate=pl.CostEstimate(
            flops=2 * rows * depth * width * n + 8 * rows * wide * depth,
            bytes_accessed=2 * (depth * width * n + 2 * wide * depth),
            transcendentals=0,
        ),
    )(
        att, code, output_projection_weight, down_rows, up_rows,
    )


def solution(mesh):
    in_specs = (
        P(("parts", "dp"), "tensor"),
        P(("parts", "dp"), "tensor", None),
        P(("parts", "dp"), None, "tensor", None),
        P("tensor", None),
        P("tensor", "dp", None),
        P("dp", None, "tensor"),
        P("parts"),
        P(),
    )
    out_specs = P(("parts", "dp"), "tensor")
    return jax.shard_map(
        functools.partial(on_device, mesh.shape["tensor"]),
        mesh=mesh,
        in_specs=in_specs,
        out_specs=out_specs,
        check_vma=False,
    )
```
